128 devices in a mesh: dap: 16 (over z, y_hi, core), ch: 8 (over y_lo, x).
Axes of the slice: x: 4, y: 4 (y_hi: 2, y_lo: 2; y = y_hi * 2 + y_lo), z: 4, core: 2. Of those that a mesh axis runs over, the one named last changes fastest.
Arguments:
- homolog_matrix_entering: bfloat16 [128, 1024, 256], P('ch', 'dap'), may hold values from -6 to 6
- attention_increment_undropped: bfloat16 [128, 1024, 256], P('ch', 'dap'), may hold values from -6 to 6
- retained_entries_indicator: int32 [1024, 256], P('dap'), may hold values 0 or 1
- pair: bfloat16 [128, 1024, 1024], P(None, 'dap', 'ch'), may hold values from -6 to 6
- pair_keep_mask: int32 [128, 1024], P(None, 'ch'), may hold values 0 or 1
- homolog_standardizing_multiplier: float32 [256], replicated, may hold values from 0.1 to 1.9
- left_right_factor_matrices: bfloat16 [256, 64], replicated, may hold values from -0.375 to 0.375
- outer_product_output_weight: bfloat16 [1024, 128], replicated, may hold values from -2 to 2
- triangle_input_gain: float32 [128], replicated, may hold values from 0.1 to 1.9
- triangle_input_weight: bfloat16 [128, 640], replicated, may hold values from -0.5 to 0.5
- triangle_output_gain: float32 [128], replicated, may hold values from 0.1 to 1.9
- triangle_output_weight: bfloat16 [128, 128], replicated, may hold values from -0.5 to 0.5
Outputs:
- pair_out: bfloat16 [128, 1024, 1024], P(None, 'dap', 'ch')
The draws below stay inside these ranges and needn't reach their ends.
All inputs are finite; a program needn't handle non-finite values. No bound on the sum of `retained_entries_indicator` or of `pair_keep_mask` on one device may be relied on, other than what follows from the above.
Results may differ from the reference program's by a relative error of at most 0.011.
Values may be sent and summed in bfloat16 or wider, within the bound.
No kernel may reach another device: no remote copies, remote signals or barrier semaphores. Data moves between devices by JAX's collectives and lax.ppermute only.
A program may use at most 192 MiB of HBM per device.

```python
import math
import jax
import jax.numpy as jnp
from jax import lax

FEATURE_DEPTH = 256
CZ = 128
HIDDEN_FACTORS = 32
HOMOLOG_TALLY = 128
AMINO_ACID_TALLY = 1024


def place_ends(result, key, low, high):
    spot = [jax.random.randint(jax.random.fold_in(key, axis), (), 0, length) for axis, length in enumerate(result.shape)]
    main_axis = result.shape.index(max(result.shape))
    neighbour = spot[:main_axis] + [(spot[main_axis] + 1) % result.shape[main_axis]] + spot[main_axis + 1:]
    return result.at[tuple(spot)].set(low).at[tuple(neighbour)].set(high)


def levels(key, shape, shards, low, largest):
    loudness = 1.0
    for position, shards_of in shards:
        steps = jax.random.uniform(jax.random.fold_in(jax.random.fold_in(key, 6), position), (shards_of,), jnp.float32, low / len(shards), largest / len(shards))
        loudness = loudness * jnp.repeat(jnp.exp(steps), shape[position] // shards_of).reshape((-1,) + (1,) * (len(shape) - 1 - position))
    return loudness


def normal_values(key, shape, scale, reach, cuts=(), kind=jnp.bfloat16):
    array = jax.random.normal(key, shape, jnp.float32) * scale
    if len(cuts) > 0:
        array = levels(key, shape, cuts, -0.22, 0.18) * array
    return jnp.clip(array, min=-reach, max=reach).astype(kind)


def setup_inputs(seed: int = 0) -> dict:
    splits = jax.random.split(jax.random.key(seed), 13)
    homolog_matrix_entering = normal_values(splits[0], (HOMOLOG_TALLY, AMINO_ACID_TALLY, FEATURE_DEPTH), 1.0, 6.0, ((0, 8), (1, 16)))
    attention_increment_undropped = normal_values(splits[1], (HOMOLOG_TALLY, AMINO_ACID_TALLY, FEATURE_DEPTH), 1.0, 6.0, ((0, 8), (1, 16)))
    retained_entries_indicator = place_ends((jax.random.randint(splits[2], (AMINO_ACID_TALLY, FEATURE_DEPTH), 0, 100) < 85).astype(jnp.int32), jax.random.fold_in(splits[2], 1), 0, 1)
    pair = normal_values(splits[3], (CZ, AMINO_ACID_TALLY, AMINO_ACID_TALLY), 1.0, 6.0, ((1, 16), (2, 8)))
    pair_keep_mask = place_ends((jax.random.randint(splits[4], (CZ, AMINO_ACID_TALLY), 0, 100) < 75).astype(jnp.int32), jax.random.fold_in(splits[4], 1), 0, 1)
    homolog_standardizing_multiplier = jnp.clip(1.0 + 0.18 * jax.random.normal(splits[5], (FEATURE_DEPTH,), jnp.float32), 0.1, 1.9)
    left_right_factor_matrices = normal_values(splits[6], (FEATURE_DEPTH, 2 * HIDDEN_FACTORS), FEATURE_DEPTH ** -0.5, 0.375)
    outer_product_output_weight = normal_values(splits[7], (HIDDEN_FACTORS * HIDDEN_FACTORS, CZ), (HIDDEN_FACTORS * HIDDEN_FACTORS // HOMOLOG_TALLY) ** -0.5, 2.0)
    triangle_input_gain = jnp.clip(1.0 + 0.18 * jax.random.normal(splits[8], (CZ,), jnp.float32), 0.1, 1.9)
    triangle_input_weight = normal_values(splits[9], (CZ, 5 * CZ), CZ ** -0.5, 0.5)
    triangle_output_gain = jnp.clip(1.0 + 0.18 * jax.random.normal(splits[10], (CZ,), jnp.float32), 0.1, 1.9)
    triangle_output_weight = normal_values(splits[11], (CZ, CZ), CZ ** -0.5, 0.5)
    return {"homolog_matrix_entering": homolog_matrix_entering, "attention_increment_undropped": attention_increment_undropped, "retained_entries_indicator": retained_entries_indicator, "pair": pair, "pair_keep_mask": pair_keep_mask, "homolog_standardizing_multiplier": homolog_standardizing_multiplier, "left_right_factor_matrices": left_right_factor_matrices, "outer_product_output_weight": outer_product_output_weight, "triangle_input_gain": triangle_input_gain, "triangle_input_weight": triangle_input_weight, "triangle_output_gain": triangle_output_gain, "triangle_output_weight": triangle_output_weight}


def layer_norm_trailing(values, gain):
    center = values - lax.optimization_barrier(jnp.mean(values, axis=-1, keepdims=True))
    spread = lax.optimization_barrier(jnp.mean(center * center, axis=-1, keepdims=True))
    return center * lax.rsqrt(spread + 1e-05) * gain

def norm_first(values, gain):
    center = values - lax.optimization_barrier(jnp.mean(values, axis=0, keepdims=True))
    spread = lax.optimization_barrier(jnp.mean(center * center, axis=0, keepdims=True))
    return center * lax.rsqrt(spread + 1e-05) * gain[:, None, None]

def reference(homolog_matrix_entering, attention_increment_undropped, retained_entries_indicator, pair, pair_keep_mask, homolog_standardizing_multiplier, left_right_factor_matrices, outer_product_output_weight, triangle_input_gain, triangle_input_weight, triangle_output_gain, triangle_output_weight):
    highest_precision = lax.Precision.HIGHEST
    dropout_scale = retained_entries_indicator.astype(jnp.float32) / 0.85
    alignment_residual_sum = homolog_matrix_entering.astype(jnp.float32) + dropout_scale[None] * attention_increment_undropped.astype(jnp.float32)
    alignment_normalized = layer_norm_trailing(alignment_residual_sum, homolog_standardizing_multiplier).astype(jnp.bfloat16)
    projected_operands = jnp.einsum('ted,dx->tex', alignment_normalized.astype(jnp.float32), left_right_factor_matrices.astype(jnp.float32), precision=highest_precision).astype(jnp.bfloat16)
    left_side = projected_operands[:, :, :HIDDEN_FACTORS].reshape(HOMOLOG_TALLY, AMINO_ACID_TALLY * HIDDEN_FACTORS)
    right_side = projected_operands[:, :, HIDDEN_FACTORS:].reshape(HOMOLOG_TALLY, AMINO_ACID_TALLY * HIDDEN_FACTORS)
    out_weights = outer_product_output_weight.astype(jnp.float32).reshape(HIDDEN_FACTORS, HIDDEN_FACTORS, CZ)
    row_block = math.gcd(AMINO_ACID_TALLY, 64)
    block_count = AMINO_ACID_TALLY // row_block

    def outer_block(block_index):
        rows_part = lax.dynamic_slice_in_dim(left_side, block_index * (row_block * HIDDEN_FACTORS), row_block * HIDDEN_FACTORS, 1)
        outer = lax.dot_general(rows_part, right_side, (((0,), (0,)), ((), ())), preferred_element_type=jnp.float32)
        outer = lax.optimization_barrier((outer / HOMOLOG_TALLY).astype(jnp.bfloat16)).astype(jnp.float32)
        outer = outer.reshape(row_block, HIDDEN_FACTORS, AMINO_ACID_TALLY, HIDDEN_FACTORS)
        return jnp.einsum('icjd,cdo->oij', outer, out_weights, precision=highest_precision)
    blocks = lax.map(outer_block, jnp.arange(block_count, dtype=jnp.int32))
    outer_mean = jnp.moveaxis(blocks, 0, 1).reshape(CZ, AMINO_ACID_TALLY, AMINO_ACID_TALLY)
    pair_mid = (pair.astype(jnp.float32) + outer_mean).astype(jnp.bfloat16)
    tri_weights = triangle_input_weight.astype(jnp.float32)

    def project_block(block_index):
        slab = lax.dynamic_slice_in_dim(pair_mid, block_index * row_block, row_block, 1).astype(jnp.float32)
        normed = lax.optimization_barrier(norm_first(slab, triangle_input_gain).astype(jnp.bfloat16)).astype(jnp.float32)
        mixed = jnp.einsum('cij,co->oij', normed, tri_weights, precision=highest_precision)
        left_value, left_gate, right_value, right_gate, out_gate = jnp.split(mixed, 5, axis=0)
        left_act = (jax.nn.sigmoid(left_gate) * left_value).astype(jnp.bfloat16)
        right_act = (jax.nn.sigmoid(right_gate) * right_value).astype(jnp.bfloat16)
        gate_act = jax.nn.sigmoid(out_gate).astype(jnp.bfloat16)
        return (left_act, right_act, gate_act)
    left_blocks, right_blocks, gate_blocks = lax.map(project_block, jnp.arange(block_count, dtype=jnp.int32))
    left_all = jnp.moveaxis(left_blocks, 0, 1).reshape(CZ, AMINO_ACID_TALLY, AMINO_ACID_TALLY)
    right_all = jnp.moveaxis(right_blocks, 0, 1).reshape(CZ, AMINO_ACID_TALLY, AMINO_ACID_TALLY)
    gate_all = jnp.moveaxis(gate_blocks, 0, 1).reshape(CZ, AMINO_ACID_TALLY, AMINO_ACID_TALLY)

    def channel_product(operands):
        return lax.dot_general(operands[0], operands[1], (((1,), (1,)), ((), ())), preferred_element_type=jnp.float32).astype(jnp.bfloat16)
    tri_sum = lax.map(channel_product, (left_all, right_all))
    pair_scale = pair_keep_mask.astype(jnp.float32) / 0.75
    final_weights = triangle_output_weight.astype(jnp.float32)

    def finish_block(block_index):
        slab = lax.dynamic_slice_in_dim(tri_sum, block_index * row_block, row_block, 1).astype(jnp.float32)
        normed = lax.optimization_barrier(norm_first(slab, triangle_output_gain).astype(jnp.bfloat16)).astype(jnp.float32)
        update = jnp.einsum('cij,co->oij', normed, final_weights, precision=highest_precision)
        gate_part = lax.dynamic_slice_in_dim(gate_all, block_index * row_block, row_block, 1).astype(jnp.float32)
        base_part = lax.dynamic_slice_in_dim(pair_mid, block_index * row_block, row_block, 1).astype(jnp.float32)
        return (base_part + pair_scale[:, None, :] * (gate_part * update)).astype(jnp.bfloat16)
    finished = lax.map(finish_block, jnp.arange(block_count, dtype=jnp.int32))
    return jnp.moveaxis(finished, 0, 1).reshape(CZ, AMINO_ACID_TALLY, AMINO_ACID_TALLY)
```

```python
import jax
import jax.numpy as jnp
from jax import lax
from jax.experimental import pallas as pl
from jax.experimental.pallas import tpu as pltpu
from jax.sharding import PartitionSpec as P

F32 = jnp.float32
BF16 = jnp.bfloat16
EPS = 1e-05
VMEM_LIMIT = 56 * 1024 * 1024
HIDDEN = 32
LANES = 128
ROWS = 64
STEP_ROWS = 16
GROUP = 4


def contract_last(a, b):
    return lax.dot_general(a, b, (((1,), (1,)), ((), ())), preferred_element_type=F32)


def params():
    return pltpu.CompilerParams(vmem_limit_bytes=VMEM_LIMIT, dimension_semantics=("arbitrary",))


def operands_kernel(homolog, increment, keep, gain, weight, out, rows_out):
    step = pl.program_id(0)
    scale = keep[...].astype(F32) / 0.85
    for t in range(2):
        parts = []
        for half in range(2):
            x = homolog[half, t].astype(F32) + scale * increment[half, t].astype(F32)
            center = x - jnp.mean(x, axis=-1, keepdims=True)
            spread = jnp.mean(center * center, axis=-1, keepdims=True)
            parts.append((center * lax.rsqrt(spread + EPS) * gain[...]).astype(BF16))
        projected = contract_last(weight[...], jnp.concatenate(parts, axis=0))
        rows_out[pl.ds(step * 2 + t, 64, stride=8), :] = projected

    @pl.when(step == pl.num_programs(0) - 1)
    def _():
        out[...] = rows_out[...].astype(BF16)


def pair_kernel(
    places, l0, l1, l2, l3, r0, r1, pair, out_weight, gain, in_weight,
    acts, mid_out, gate_out,
    l_parts, r_parts, l_rows, left, right, outer, pair_rows, left_rows, right_rows,
):
    step = pl.program_id(0)

    @pl.when(step == 0)
    def _():
        for k, block in enumerate((l0, l1, l2, l3)):
            for q in range(2):
                l_parts[places[2 * k + q]] = block[q].astype(F32).reshape(HIDDEN, 8, LANES)
        for k, block in enumerate((r0, r1)):
            for q in range(8):
                r_parts[places[8 + 8 * k + q]] = block[q].astype(F32).reshape(HIDDEN, 8, LANES)
        for c in range(HIDDEN):
            turned = l_parts[:, c].reshape(64, LANES).T
            l_rows[pl.ds(c, ROWS, stride=HIDDEN), :] = jnp.concatenate([turned[:64], turned[64:]], axis=1)
        left[...] = l_rows[...].astype(BF16)
        low = lax.broadcasted_iota(jnp.int32, (64, LANES), 1) < 64
        for d in range(HIDDEN):
            a0 = r_parts[0:8, d].reshape(64, LANES)
            a1 = r_parts[8:16, d].reshape(64, LANES)
            first = jnp.where(low, a0, pltpu.roll(a1, 64, 1))
            second = jnp.where(low, pltpu.roll(a0, 64, 1), a1)
            right[:, d * LANES:(d + 1) * LANES] = jnp.concatenate([first, second], axis=0).astype(BF16)

    pair_rows[...] = pair[...].astype(F32).reshape(LANES * STEP_ROWS, LANES)
    rows = left[pl.ds(pl.multiple_of(step * (STEP_ROWS * HIDDEN), STEP_ROWS * HIDDEN), STEP_ROWS * HIDDEN), :]
    for n in range(16):
        product = jnp.dot(rows, right[:, n * 256:(n + 1) * 256], preferred_element_type=F32).astype(BF16)
        for i in range(STEP_ROWS):
            for q in range(2):
                d = 2 * n + q
                outer[d * HIDDEN:(d + 1) * HIDDEN, i * LANES:(i + 1) * LANES] = product[
                    i * HIDDEN:(i + 1) * HIDDEN, q * LANES:(q + 1) * LANES
                ]
    for g in range(STEP_ROWS // GROUP):
        mean_part = jnp.dot(
            out_weight[...], outer[:, g * GROUP * LANES:(g + 1) * GROUP * LANES], preferred_element_type=F32
        ) * (1.0 / 128.0)
        base = jnp.concatenate(
            [pair_rows[pl.ds(g * GROUP + t, LANES, stride=STEP_ROWS), :] for t in range(GROUP)], axis=1
        )
        mid = (base + mean_part).astype(BF16)
        for t in range(GROUP):
            mid_out[g * GROUP + t] = mid[:, t * LANES:(t + 1) * LANES]
        x = mid.astype(F32)
        center = x - jnp.mean(x, axis=0, keepdims=True)
        spread = jnp.mean(center * center, axis=0, keepdims=True)
        normed = (center * lax.rsqrt(spread + EPS) * gain[...]).astype(BF16)
        mixed = jnp.dot(in_weight[...], normed, preferred_element_type=F32)
        left_act = jax.nn.sigmoid(mixed[128:256]) * mixed[0:128]
        right_act = jax.nn.sigmoid(mixed[384:512]) * mixed[256:384]
        gate_act = jax.nn.sigmoid(mixed[512:640]).astype(BF16)
        for t in range(GROUP):
            i = g * GROUP + t
            lanes = slice(t * LANES, (t + 1) * LANES)
            left_rows[pl.ds(i, LANES, stride=STEP_ROWS), :] = left_act[:, lanes]
            right_rows[pl.ds(i, LANES, stride=STEP_ROWS), :] = right_act[:, lanes]
            gate_out[i] = gate_act[:, lanes]
    acts[:, 0] = left_rows[...].reshape(LANES, STEP_ROWS, LANES).astype(BF16)
    acts[:, 1] = right_rows[...].reshape(LANES, STEP_ROWS, LANES).astype(BF16)


def triangle_kernel(left_all, right_some, out, left, right):
    @pl.when(pl.program_id(0) == 0)
    def _():
        for d in range(16):
            for h in range(8):
                left[d * 64:(d + 1) * 64, h * LANES:(h + 1) * LANES] = left_all[d, h, 0]

    for d in range(4):
        for h in range(8):
            right[d * 64:(d + 1) * 64, h * LANES:(h + 1) * LANES] = right_some[d, h, 0]
    for m in range(4):
        product = contract_last(left[m * 256:(m + 1) * 256, :], right[...]).astype(BF16)
        for d in range(4):
            for h in range(2):
                out[m * 4 + d, h] = product[d * 64:(d + 1) * 64, h * LANES:(h + 1) * LANES]


def finish_kernel(tri, mid, gate, keep, gain, weight, out, tri_rows, out_rows):
    tri_rows[...] = tri[...].astype(F32).reshape(LANES * STEP_ROWS, LANES)
    scale = keep[...].astype(F32) / 0.75
    for g in range(STEP_ROWS // GROUP):
        x = jnp.concatenate(
            [tri_rows[pl.ds(g * GROUP + t, LANES, stride=STEP_ROWS), :] for t in range(GROUP)], axis=1
        )
        center = x - jnp.mean(x, axis=0, keepdims=True)
        spread = jnp.mean(center * center, axis=0, keepdims=True)
        normed = (center * lax.rsqrt(spread + EPS) * gain[...]).astype(BF16)
        update = jnp.dot(weight[...], normed, preferred_element_type=F32)
        for t in range(GROUP):
            i = g * GROUP + t
            part = update[:, t * LANES:(t + 1) * LANES]
            out_rows[pl.ds(i, LANES, stride=STEP_ROWS), :] = mid[i].astype(F32) + scale * (
                gate[i].astype(F32) * part
            )
    out[...] = out_rows[...].reshape(LANES, STEP_ROWS, LANES).astype(BF16)


def whole(shape):
    return pl.BlockSpec(shape, lambda i: (0,) * len(shape))


def on_device(
    homolog_matrix_entering,
    attention_increment_undropped,
    retained_entries_indicator,
    pair,
    pair_keep_mask,
    homolog_standardizing_multiplier,
    left_right_factor_matrices,
    outer_product_output_weight,
    triangle_input_gain,
    triangle_input_weight,
    triangle_output_gain,
    triangle_output_weight,
):
    dap, ch = lax.axis_index("dap"), lax.axis_index("ch")
    operands = pl.pallas_call(
        operands_kernel,
        grid=(4,),
        out_shape=jax.ShapeDtypeStruct((512, LANES), BF16),
        in_specs=[
            pl.BlockSpec((2, 2, ROWS, 256), lambda i: (0, i, 0, 0)),
            pl.BlockSpec((2, 2, ROWS, 256), lambda i: (0, i, 0, 0)),
            whole((ROWS, 256)),
            whole((1, 256)),
            whole((64, 256)),
        ],
        out_specs=whole((512, LANES)),
        scratch_shapes=[pltpu.VMEM((512, LANES), F32)],
        compiler_params=params(),
        name="operands",
    )(
        homolog_matrix_entering.reshape(2, 8, ROWS, 256),
        attention_increment_undropped.reshape(2, 8, ROWS, 256),
        retained_entries_indicator,
        homolog_standardizing_multiplier.reshape(1, 256),
        left_right_factor_matrices.T,
    )
    left_block, right_block = operands[None, :256], operands[None, 256:]

    both = ("dap", "ch")

    def turn(flip):
        return [(d * 8 + h, (((d % 2) * 8 + h) ^ flip) * 8 + d // 2) for d in range(16) for h in range(8)]

    r_own = lax.ppermute(right_block, both, turn(0))
    r_flip = lax.ppermute(right_block, both, turn(2))
    l_flip = lax.ppermute(left_block, "ch", [(i, i ^ 4) for i in range(8)])
    r_pair = jnp.concatenate([r_own, r_flip], axis=0)
    l_pair = jnp.concatenate([left_block, l_flip], axis=0)
    r_quads = [r_pair] + [
        lax.ppermute(r_pair, "dap", [(i, (i + 4 * k) % 16) for i in range(16)]) for k in range(1, 4)
    ]
    l_quads = [l_pair] + [
        lax.ppermute(l_pair, "ch", [(i, (i & 4) | ((i + k) & 3)) for i in range(8)]) for k in range(1, 4)
    ]
    r_half = jnp.concatenate(r_quads, axis=0)
    r_other = lax.ppermute(r_half, "dap", [(i, i ^ 1) for i in range(16)])
    places = []
    for k in range(4):
        spot = (ch & 4) | ((ch - k) & 3)
        places += [spot, spot ^ 4]
    for core in range(2):
        for k in range(4):
            spot = ((dap ^ core) - 4 * k) & 15
            places += [spot, spot ^ 2]
    places = jnp.stack(places).astype(jnp.int32)

    acts, pair_mid, gate = pl.pallas_call(
        pair_kernel,
        grid=(ROWS // STEP_ROWS,),
        out_shape=(
            jax.ShapeDtypeStruct((LANES, 2, ROWS, LANES), BF16),
            jax.ShapeDtypeStruct((ROWS, LANES, LANES), BF16),
            jax.ShapeDtypeStruct((ROWS, LANES, LANES), BF16),
        ),
        in_specs=[pl.BlockSpec(memory_space=pltpu.SMEM)]
        + [whole((2, 256, LANES))] * 4
        + [whole((8, 256, LANES))] * 2
        + [
            pl.BlockSpec((LANES, STEP_ROWS, LANES), lambda i: (0, i, 0)),
            whole((LANES, 1024)),
            whole((LANES, 1)),
            whole((640, LANES)),
        ],
        out_specs=(
            pl.BlockSpec((LANES, 2, STEP_ROWS, LANES), lambda i: (0, 0, i, 0)),
            pl.BlockSpec((STEP_ROWS, LANES, LANES), lambda i: (i, 0, 0)),
            pl.BlockSpec((STEP_ROWS, LANES, LANES), lambda i: (i, 0, 0)),
        ),
        scratch_shapes=[
            pltpu.VMEM((8, HIDDEN, 8, LANES), F32),
            pltpu.VMEM((16, HIDDEN, 8, LANES), F32),
            pltpu.VMEM((ROWS * HIDDEN, LANES), F32),
            pltpu.VMEM((ROWS * HIDDEN, LANES), BF16),
            pltpu.VMEM((LANES, HIDDEN * LANES), BF16),
            pltpu.VMEM((1024, STEP_ROWS * LANES), BF16),
            pltpu.VMEM((LANES * STEP_ROWS, LANES), F32),
            pltpu.VMEM((LANES * STEP_ROWS, LANES), F32),
            pltpu.VMEM((LANES * STEP_ROWS, LANES), F32),
        ],
        compiler_params=params(),
        name="pair_update",
    )(
        places,
        *l_quads,
        r_half,
        r_other,
        pair,
        outer_product_output_weight.reshape(HIDDEN, HIDDEN, LANES).transpose(2, 1, 0).reshape(LANES, 1024),
        triangle_input_gain.reshape(LANES, 1),
        triangle_input_weight.T,
    )
    acts = lax.all_to_all(acts.reshape(LANES, LANES, LANES), both, 0, 0, tiled=True)
    acts = acts.reshape(16, 8, 2, ROWS, LANES)

    tri = pl.pallas_call(
        triangle_kernel,
        grid=(4,),
        out_shape=jax.ShapeDtypeStruct((16, 8, ROWS, LANES), BF16),
        in_specs=[
            pl.BlockSpec((16, 8, 1, ROWS, LANES), lambda i: (0, 0, 0, 0, 0)),
            pl.BlockSpec((4, 8, 1, ROWS, LANES), lambda i: (i, 0, 1, 0, 0)),
        ],
        out_specs=pl.BlockSpec((16, 2, ROWS, LANES), lambda i: (0, i, 0, 0)),
        scratch_shapes=[pltpu.VMEM((1024, 1024), BF16), pltpu.VMEM((256, 1024), BF16)],
        compiler_params=params(),
        name="triangle",
    )(acts, acts)
    tri = lax.all_to_all(tri.reshape(LANES, ROWS, LANES), both, 0, 0, tiled=True)

    return pl.pallas_call(
        finish_kernel,
        grid=(ROWS // STEP_ROWS,),
        out_shape=jax.ShapeDtypeStruct((LANES, ROWS, LANES), BF16),
        in_specs=[
            pl.BlockSpec((LANES, STEP_ROWS, LANES), lambda i: (0, i, 0)),
            pl.BlockSpec((STEP_ROWS, LANES, LANES), lambda i: (i, 0, 0)),
            pl.BlockSpec((STEP_ROWS, LANES, LANES), lambda i: (i, 0, 0)),
            whole((LANES, LANES)),
            whole((LANES, 1)),
            whole((LANES, LANES)),
        ],
        out_specs=pl.BlockSpec((LANES, STEP_ROWS, LANES), lambda i: (0, i, 0)),
        scratch_shapes=[
            pltpu.VMEM((LANES * STEP_ROWS, LANES), F32),
            pltpu.VMEM((LANES * STEP_ROWS, LANES), F32),
        ],
        compiler_params=params(),
        name="finish",
    )(
        tri,
        pair_mid,
        gate,
        pair_keep_mask,
        triangle_output_gain.reshape(LANES, 1),
        triangle_output_weight.T,
    )


def solution(mesh):
    placed = (
        P("ch", "dap", None),
        P("ch", "dap", None),
        P("dap", None),
        P(None, "dap", "ch"),
        P(None, "ch"),
        P(),
        P(),
        P(),
        P(),
        P(),
        P(),
        P(),
    )
    return jax.shard_map(
        on_device, mesh=mesh, in_specs=placed, out_specs=P(None, "dap", "ch"), check_vma=False
    )
```

```python
import jax
import jax.numpy as jnp
from jax import lax
from jax.experimental import pallas as pl
from jax.experimental.pallas import tpu as pltpu
from jax.sharding import PartitionSpec as P

F32 = jnp.float32
BF16 = jnp.bfloat16
EPS = 1e-05
MIB = 1024 * 1024
HIDDEN = 32
LANES = 128
ROWS = 64
STEP_ROWS = 16
PITCH = 24
GROUP = 8


def contract_last(a, b):
    return lax.dot_general(a, b, (((1,), (1,)), ((), ())), preferred_element_type=F32)


def params(mib):
    return pltpu.CompilerParams(vmem_limit_bytes=mib * MIB, dimension_semantics=("arbitrary",))


def resident(x):
    return pltpu.with_memory_space_constraint(x, pltpu.VMEM)


def in_hbm(x):
    return pltpu.with_memory_space_constraint(x, pltpu.HBM)


IN_VMEM = pl.BlockSpec(memory_space=pltpu.VMEM)


def operands_kernel(homolog, increment, keep, gain, weight, left_out, right_out, rows_out):
    step = pl.program_id(0)
    scale = keep[...].astype(F32) / 0.85
    for t in range(2):
        parts = []
        for half in range(2):
            x = homolog[half, t].astype(F32) + scale * increment[half, t].astype(F32)
            center = x - jnp.mean(x, axis=-1, keepdims=True)
            spread = jnp.mean(center * center, axis=-1, keepdims=True)
            parts.append((center * lax.rsqrt(spread + EPS) * gain[...]).astype(BF16))
        projected = contract_last(weight[...], jnp.concatenate(parts, axis=0))
        rows_out[pl.ds(step * 2 + t, 64, stride=8), :] = projected

    @pl.when(step == pl.num_programs(0) - 1)
    def _():
        left_out[...] = jnp.broadcast_to(rows_out[0:256, :].astype(BF16), (8, 256, LANES))
        right_out[...] = rows_out[256:512, :].astype(BF16)


def spread_rows(rows, values):
    for c in range(LANES):
        rows[c * PITCH:c * PITCH + STEP_ROWS, :] = values[c]


def gather_rows(rows):
    return rows[...].reshape(LANES, PITCH, LANES)[:, :STEP_ROWS].astype(BF16)


def weights_kernel(
    out_weight, in_weight, in_gain, tri_gain, tri_weight,
    out_turned, in_turned, in_column, tri_column, tri_turned,
):
    w = out_weight[...].astype(F32).reshape(HIDDEN, HIDDEN, LANES)
    for d in range(HIDDEN // 4):
        rows = jnp.concatenate([w[:, 4 * d + q, :] for q in range(4)], axis=0)
        out_turned[:, d * LANES:(d + 1) * LANES] = rows.T.astype(BF16)
    for k in range(5):
        in_turned[k * LANES:(k + 1) * LANES, :] = in_weight[:, k * LANES:(k + 1) * LANES].astype(F32).T.astype(BF16)
    tri_turned[...] = tri_weight[...].astype(F32).T.astype(BF16)
    in_column[...] = jnp.broadcast_to(in_gain[...], (8, LANES)).T[:, 0:1]
    tri_column[...] = jnp.broadcast_to(tri_gain[...], (8, LANES)).T[:, 0:1]


def pair_kernel(
    place, l_all, r_half, r_other, pair, out_weight, gain, in_weight,
    acts, mid_out, normed_out,
    l_parts, r_parts, l_rows, left, right, outer_a, outer_b, pair_rows, left_rows, right_rows, weight_here, sem,
):
    fetch = pltpu.make_async_copy(out_weight, weight_here, sem)
    fetch.start()
    for q in range(8):
        l_parts[q] = l_all[q].astype(F32).reshape(HIDDEN, 8, LANES)
        for other, blocks in enumerate((r_half, r_other)):
            spot = (((place[0] ^ other) - 4 * (q // 2)) & 15) ^ (2 * (q % 2))
            r_parts[(spot & 1) * 8 + (spot >> 1)] = blocks[q].astype(F32).reshape(HIDDEN, 8, LANES)
    for c in range(HIDDEN):
        turned = l_parts[:, c].reshape(64, LANES).T
        l_rows[pl.ds(c, ROWS, stride=HIDDEN + 8), :] = jnp.concatenate([turned[:64], turned[64:]], axis=1)
    left[...] = l_rows[...].reshape(ROWS, HIDDEN + 8, LANES)[:, :HIDDEN].reshape(ROWS * HIDDEN, LANES).astype(BF16)
    low = lax.broadcasted_iota(jnp.int32, (64, LANES), 1) < 64
    for d in range(HIDDEN):
        a0 = r_parts[0:8, d].reshape(64, LANES)
        a1 = r_parts[8:16, d].reshape(64, LANES)
        first = jnp.where(low, a0, pltpu.roll(a1, 64, 1))
        second = jnp.where(low, pltpu.roll(a0, 64, 1), a1)
        right[:, d * LANES:(d + 1) * LANES] = jnp.concatenate([first, second], axis=0).astype(BF16)

    outers = (outer_a, outer_b)
    steps = ROWS // STEP_ROWS

    def outer_product(step, chunks):
        if step >= steps:
            return
        outer = outers[step % 2]
        rows = left[step * STEP_ROWS * HIDDEN:(step + 1) * STEP_ROWS * HIDDEN, :]
        for n in chunks:
            product = jnp.dot(rows, right[:, n * 256:(n + 1) * 256], preferred_element_type=F32).astype(BF16)
            for i in range(STEP_ROWS):
                for q in range(2):
                    d = 2 * n + q
                    outer[d * HIDDEN:(d + 1) * HIDDEN, i * LANES:(i + 1) * LANES] = product[
                        i * HIDDEN:(i + 1) * HIDDEN, q * LANES:(q + 1) * LANES
                    ]

    def update(step, g):
        mean_part = jnp.dot(
            weight_here[...], outers[step % 2][:, g * GROUP * LANES:(g + 1) * GROUP * LANES],
            preferred_element_type=F32,
        ) * (1.0 / 128.0)
        base = jnp.concatenate(
            [pair_rows[pl.ds(g * GROUP + t, LANES, stride=PITCH), :] for t in range(GROUP)], axis=1
        )
        mid = (base + mean_part).astype(BF16)
        x = mid.astype(F32)
        center = x - jnp.mean(x, axis=0, keepdims=True)
        spread = jnp.mean(center * center, axis=0, keepdims=True)
        normed = (center * lax.rsqrt(spread + EPS) * gain[...]).astype(BF16)
        for t in range(GROUP):
            i = step * STEP_ROWS + g * GROUP + t
            mid_out[i] = mid[:, t * LANES:(t + 1) * LANES]
            normed_out[i] = normed[:, t * LANES:(t + 1) * LANES]
        return normed

    def activate(g, normed):
        mixed = jnp.dot(in_weight[0:512, :], normed, preferred_element_type=F32)
        left_act = jax.nn.sigmoid(mixed[128:256]) * mixed[0:128]
        right_act = jax.nn.sigmoid(mixed[384:512]) * mixed[256:384]
        for t in range(GROUP):
            i = g * GROUP + t
            lanes = slice(t * LANES, (t + 1) * LANES)
            left_rows[pl.ds(i, LANES, stride=PITCH), :] = left_act[:, lanes]
            right_rows[pl.ds(i, LANES, stride=PITCH), :] = right_act[:, lanes]

    outer_product(0, range(16))
    fetch.wait()
    groups = STEP_ROWS // GROUP
    share = 16 // (2 * groups)
    for step in range(steps):
        here = slice(step * STEP_ROWS, (step + 1) * STEP_ROWS)
        spread_rows(pair_rows, pair[:, here, :].astype(F32))
        for g in range(groups):
            normed = update(step, g)
            outer_product(step + 1, range(2 * g * share, (2 * g + 1) * share))
            activate(g, normed)
            outer_product(step + 1, range((2 * g + 1) * share, (2 * g + 2) * share))
        acts[:, 0, here, :] = gather_rows(left_rows)
        acts[:, 1, here, :] = gather_rows(right_rows)


def triangle_kernel(acts, out):
    def rows(block, side):
        return jnp.concatenate([acts[block * 8 + h, side] for h in range(8)], axis=1)

    for n in range(4):
        right = jnp.concatenate([rows(n * 4 + d, 1) for d in range(4)], axis=0)
        for m in range(4):
            left = jnp.concatenate([rows(m * 4 + d, 0) for d in range(4)], axis=0)
            product = contract_last(left, right).astype(BF16)
            for d in range(4):
                for h in range(2):
                    out[(m * 4 + d) * 8 + n * 2 + h] = product[d * 64:(d + 1) * 64, h * LANES:(h + 1) * LANES]


def finish_kernel(tri, mid, pair_normed, keep, gain, weight, gate_weight, out, tri_rows, out_rows):
    scale = keep[...].astype(F32) / 0.75
    first = pl.multiple_of(pl.program_id(0) * STEP_ROWS, STEP_ROWS)
    spread_rows(tri_rows, tri[:, pl.ds(first, STEP_ROWS), :].astype(F32))
    for g in range(STEP_ROWS // GROUP):
        x = jnp.concatenate(
            [tri_rows[pl.ds(g * GROUP + t, LANES, stride=PITCH), :] for t in range(GROUP)], axis=1
        )
        center = x - jnp.mean(x, axis=0, keepdims=True)
        spread = jnp.mean(center * center, axis=0, keepdims=True)
        normed = (center * lax.rsqrt(spread + EPS) * gain[...]).astype(BF16)
        update = jnp.dot(weight[...], normed, preferred_element_type=F32)
        gate = jnp.dot(
            gate_weight[512:640, :],
            jnp.concatenate([pair_normed[first + g * GROUP + t] for t in range(GROUP)], axis=1),
            preferred_element_type=F32,
        )
        update = jax.nn.sigmoid(gate).astype(BF16).astype(F32) * update
        for t in range(GROUP):
            i = g * GROUP + t
            out_rows[pl.ds(i, LANES, stride=PITCH), :] = (
                mid[first + i].astype(F32) + scale * update[:, t * LANES:(t + 1) * LANES]
            )
    out[...] = gather_rows(out_rows)


def whole(shape):
    return pl.BlockSpec(shape, lambda i: (0,) * len(shape))


def on_device(
    homolog_matrix_entering,
    attention_increment_undropped,
    retained_entries_indicator,
    pair,
    pair_keep_mask,
    homolog_standardizing_multiplier,
    left_right_factor_matrices,
    outer_product_output_weight,
    triangle_input_gain,
    triangle_input_weight,
    triangle_output_gain,
    triangle_output_weight,
):
    left_blocks, right_block = pl.pallas_call(
        operands_kernel,
        grid=(4,),
        out_shape=(jax.ShapeDtypeStruct((8, 256, LANES), BF16), jax.ShapeDtypeStruct((256, LANES), BF16)),
        in_specs=[
            pl.BlockSpec((2, 2, ROWS, 256), lambda i: (0, i, 0, 0)),
            pl.BlockSpec((2, 2, ROWS, 256), lambda i: (0, i, 0, 0)),
            whole((ROWS, 256)),
            whole((1, 256)),
            whole((64, 256)),
        ],
        out_specs=(whole((8, 256, LANES)), whole((256, LANES))),
        scratch_shapes=[pltpu.VMEM((512, LANES), F32)],
        compiler_params=params(16),
        name="operands",
    )(
        in_hbm(homolog_matrix_entering.reshape(2, 8, ROWS, 256)),
        in_hbm(attention_increment_undropped.reshape(2, 8, ROWS, 256)),
        in_hbm(retained_entries_indicator),
        in_hbm(homolog_standardizing_multiplier.reshape(1, 256)),
        in_hbm(left_right_factor_matrices.T),
    )
    both = ("dap", "ch")
    turn = [(d * 8 + h, (h * 2 + d % 2) * 8 + d // 2) for d in range(16) for h in range(8)]
    right_block = lax.ppermute(right_block[None], both, turn)
    raw = lax.optimization_barrier(
        (
            outer_product_output_weight,
            triangle_input_weight,
            triangle_input_gain.reshape(1, LANES),
            triangle_output_gain.reshape(1, LANES),
            triangle_output_weight,
            left_blocks,
        )
    )
    turned = pl.pallas_call(
        weights_kernel,
        out_shape=(
            jax.ShapeDtypeStruct((LANES, 1024), BF16),
            pltpu.VMEM((640, LANES), BF16),
            pltpu.VMEM((LANES, 1), F32),
            pltpu.VMEM((LANES, 1), F32),
            pltpu.VMEM((LANES, LANES), BF16),
        ),
        in_specs=[IN_VMEM] * 5,
        out_specs=(IN_VMEM,) * 5,
        compiler_params=pltpu.CompilerParams(vmem_limit_bytes=8 * MIB),
        name="weights",
    )(*[in_hbm(x) for x in raw[:5]])
    l_all = lax.all_to_all(left_blocks, "ch", 0, 0, tiled=True)
    right_block, l_all, turned = lax.optimization_barrier((right_block, l_all, turned))
    r_flip = lax.ppermute(right_block, "dap", [(i, i ^ 2) for i in range(16)])
    r_pair = jnp.concatenate([right_block, r_flip], axis=0)
    quads = [r_pair] + [lax.ppermute(r_pair, "dap", [(i, (i + 4 * k) % 16) for i in range(16)]) for k in range(1, 4)]
    r_half = jnp.concatenate(quads, axis=0)
    r_other = lax.ppermute(r_half, "dap", [(i, i ^ 1) for i in range(16)])
    out_weight, in_weight, in_gain, tri_gain, tri_weight = turned
    place = lax.axis_index("dap").astype(jnp.int32).reshape(1)

    acts, pair_mid, normed = pl.pallas_call(
        pair_kernel,
        out_shape=(
            pltpu.VMEM((LANES, 2, ROWS, LANES), BF16),
            pltpu.VMEM((ROWS, LANES, LANES), BF16),
            pltpu.VMEM((ROWS, LANES, LANES), BF16),
        ),
        in_specs=[pl.BlockSpec(memory_space=pltpu.SMEM)]
        + [IN_VMEM] * 4
        + [pl.BlockSpec(memory_space=pl.ANY)]
        + [IN_VMEM] * 2,
        out_specs=(IN_VMEM,) * 3,
        scratch_shapes=[
            pltpu.VMEM((8, HIDDEN, 8, LANES), F32),
            pltpu.VMEM((16, HIDDEN, 8, LANES), F32),
            pltpu.VMEM((ROWS * (HIDDEN + 8), LANES), F32),
            pltpu.VMEM((ROWS * HIDDEN, LANES), BF16),
            pltpu.VMEM((LANES, HIDDEN * LANES), BF16),
            pltpu.VMEM((1024, STEP_ROWS * LANES), BF16),
            pltpu.VMEM((1024, STEP_ROWS * LANES), BF16),
            pltpu.VMEM((LANES * PITCH, LANES), F32),
            pltpu.VMEM((LANES * PITCH, LANES), F32),
            pltpu.VMEM((LANES * PITCH, LANES), F32),
            pltpu.VMEM((LANES, 1024), BF16),
            pltpu.SemaphoreType.DMA,
        ],
        compiler_params=pltpu.CompilerParams(vmem_limit_bytes=28 * MIB),
        name="pair_update",
    )(
        place, resident(l_all), resident(r_half), resident(r_other), resident(pair),
        in_hbm(out_weight), resident(in_gain), resident(in_weight),
    )
    acts = lax.all_to_all(acts.reshape(LANES, LANES, LANES), both, 0, 0, tiled=True)

    tri = pl.pallas_call(
        triangle_kernel,
        out_shape=pltpu.VMEM((LANES, ROWS, LANES), BF16),
        in_specs=[IN_VMEM],
        out_specs=IN_VMEM,
        compiler_params=pltpu.CompilerParams(vmem_limit_bytes=16 * MIB),
        name="triangle",
    )(resident(acts.reshape(LANES, 2, ROWS, LANES)))
    tri = lax.all_to_all(tri, both, 0, 0, tiled=True)

    return pl.pallas_call(
        finish_kernel,
        grid=(ROWS // STEP_ROWS,),
        out_shape=jax.ShapeDtypeStruct((LANES, ROWS, LANES), BF16),
        in_specs=[IN_VMEM] * 7,
        out_specs=pl.BlockSpec((LANES, STEP_ROWS, LANES), lambda i: (0, i, 0)),
        scratch_shapes=[pltpu.VMEM((LANES * PITCH, LANES), F32)] * 2,
        compiler_params=params(20),
        name="finish",
    )(
        resident(tri), resident(pair_mid), resident(normed), pair_keep_mask,
        resident(tri_gain), resident(tri_weight), resident(in_weight),
    )


def solution(mesh):
    placed = (
        P("ch", "dap", None),
        P("ch", "dap", None),
        P("dap", None),
        P(None, "dap", "ch"),
        P(None, "ch"),
        P(),
        P(),
        P(),
        P(),
        P(),
        P(),
        P(),
    )
    return jax.shard_map(
        on_device, mesh=mesh, in_specs=placed, out_specs=P(None, "dap", "ch"), check_vma=False
    )
```

```python
import jax
import jax.numpy as jnp
from jax import lax
from jax.experimental import pallas as pl
from jax.experimental.pallas import tpu as pltpu
from jax.sharding import PartitionSpec as P

F32 = jnp.float32
BF16 = jnp.bfloat16
EPS = 1e-05
MIB = 1024 * 1024
HIDDEN = 32
LANES = 128
ROWS = 64
STEP_ROWS = 16
PITCH = 24
GROUP = 8


def contract_last(a, b):
    return lax.dot_general(a, b, (((1,), (1,)), ((), ())), preferred_element_type=F32)


def params(mib):
    return pltpu.CompilerParams(vmem_limit_bytes=mib * MIB, dimension_semantics=("arbitrary",))


def resident(x):
    return pltpu.with_memory_space_constraint(x, pltpu.VMEM)


def in_hbm(x):
    return pltpu.with_memory_space_constraint(x, pltpu.HBM)


IN_VMEM = pl.BlockSpec(memory_space=pltpu.VMEM)


def operands_kernel(homolog, increment, keep, gain, weight, left_out, right_out, rows_out):
    step = pl.program_id(0)
    scale = keep[...].astype(F32) / 0.85
    for t in range(4):
        parts = []
        for half in range(2):
            x = homolog[half, t].astype(F32) + scale * increment[half, t].astype(F32)
            center = x - jnp.mean(x, axis=-1, keepdims=True)
            spread = jnp.mean(center * center, axis=-1, keepdims=True)
            parts.append((center * lax.rsqrt(spread + EPS) * gain[...]).astype(BF16))
        projected = contract_last(weight[...], jnp.concatenate(parts, axis=0))
        rows_out[pl.ds(step * 4 + t, 64, stride=8), :] = projected

    @pl.when(step == pl.num_programs(0) - 1)
    def _():
        left_out[...] = rows_out[0:256, :].astype(BF16)
        right_out[...] = rows_out[256:512, :].astype(BF16)


def spread_rows(rows, values):
    for c in range(LANES):
        rows[c * PITCH:c * PITCH + STEP_ROWS, :] = values[c]


def gather_rows(rows):
    return rows[...].reshape(LANES, PITCH, LANES)[:, :STEP_ROWS].astype(BF16)


def weights_kernel(
    out_weight, in_weight, in_gain, tri_gain, tri_weight,
    out_turned, in_turned, in_column, tri_column, tri_turned,
):
    w = out_weight[...].astype(F32).reshape(HIDDEN, HIDDEN, LANES)
    for d in range(HIDDEN // 4):
        rows = jnp.concatenate([w[:, 4 * d + q, :] for q in range(4)], axis=0)
        out_turned[:, d * LANES:(d + 1) * LANES] = rows.T.astype(BF16)
    for k in range(5):
        in_turned[k * LANES:(k + 1) * LANES, :] = in_weight[:, k * LANES:(k + 1) * LANES].astype(F32).T.astype(BF16)
    tri_turned[...] = tri_weight[...].astype(F32).T.astype(BF16)
    in_column[...] = jnp.broadcast_to(in_gain[...], (8, LANES)).T[:, 0:1]
    tri_column[...] = jnp.broadcast_to(tri_gain[...], (8, LANES)).T[:, 0:1]


def turn_left(place, quads, left, parts, rows):
    for k, blocks in enumerate(quads):
        for q in range(2):
            spot = ((place[1] & 4) | ((place[1] - k) & 3)) ^ (4 * q)
            parts[spot] = blocks[q].astype(F32).reshape(HIDDEN, 8, LANES)
    for c in range(HIDDEN):
        turned = parts[:, c].reshape(64, LANES).T
        rows[pl.ds(c, ROWS, stride=HIDDEN + 8), :] = jnp.concatenate([turned[:64], turned[64:]], axis=1)
    left[...] = rows[...].reshape(ROWS, HIDDEN + 8, LANES)[:, :HIDDEN].reshape(ROWS * HIDDEN, LANES).astype(BF16)


def pair_kernel(
    place, l0, l1, l2, l3, r_half, r_other, pair_far, out_weight, gain, in_weight,
    acts, mid_out, normed_out,
    l_parts, l_rows, left, r_parts, right, outer_a, outer_b, pair_rows, left_rows, right_rows,
    weight_here, pair, weight_sem, pair_sem,
):
    fetch_weight = pltpu.make_async_copy(out_weight, weight_here, weight_sem)
    fetch_pair = pltpu.make_async_copy(pair_far, pair, pair_sem)
    fetch_weight.start()
    fetch_pair.start()
    turn_left(place, (l0, l1, l2, l3), left, l_parts, l_rows)
    for q in range(8):
        for other, blocks in enumerate((r_half, r_other)):
            spot = (((place[0] ^ other) - 4 * (q // 2)) & 15) ^ (2 * (q % 2))
            r_parts[(spot & 1) * 8 + (spot >> 1)] = blocks[q].astype(F32).reshape(HIDDEN, 8, LANES)
    low = lax.broadcasted_iota(jnp.int32, (64, LANES), 1) < 64
    for d in range(HIDDEN):
        a0 = r_parts[0:8, d].reshape(64, LANES)
        a1 = r_parts[8:16, d].reshape(64, LANES)
        first = jnp.where(low, a0, pltpu.roll(a1, 64, 1))
        second = jnp.where(low, pltpu.roll(a0, 64, 1), a1)
        right[:, d * LANES:(d + 1) * LANES] = jnp.concatenate([first, second], axis=0).astype(BF16)

    outers = (outer_a, outer_b)
    steps = ROWS // STEP_ROWS

    def outer_product(step, chunks):
        if step >= steps:
            return
        outer = outers[step % 2]
        rows = left[step * STEP_ROWS * HIDDEN:(step + 1) * STEP_ROWS * HIDDEN, :]
        for n in chunks:
            product = jnp.dot(rows, right[:, n * 256:(n + 1) * 256], preferred_element_type=F32).astype(BF16)
            for i in range(STEP_ROWS):
                for q in range(2):
                    d = 2 * n + q
                    outer[d * HIDDEN:(d + 1) * HIDDEN, i * LANES:(i + 1) * LANES] = product[
                        i * HIDDEN:(i + 1) * HIDDEN, q * LANES:(q + 1) * LANES
                    ]

    def update(step, g):
        mean_part = jnp.dot(
            weight_here[...], outers[step % 2][:, g * GROUP * LANES:(g + 1) * GROUP * LANES],
            preferred_element_type=F32,
        ) * (1.0 / 128.0)
        base = jnp.concatenate(
            [pair_rows[pl.ds(g * GROUP + t, LANES, stride=PITCH), :] for t in range(GROUP)], axis=1
        )
        mid = (base + mean_part).astype(BF16)
        x = mid.astype(F32)
        center = x - jnp.mean(x, axis=0, keepdims=True)
        spread = jnp.mean(center * center, axis=0, keepdims=True)
        normed = (center * lax.rsqrt(spread + EPS) * gain[...]).astype(BF16)
        for t in range(GROUP):
            i = step * STEP_ROWS + g * GROUP + t
            mid_out[i] = mid[:, t * LANES:(t + 1) * LANES]
            normed_out[i] = normed[:, t * LANES:(t + 1) * LANES]
        return normed

    def activate(g, normed):
        mixed = jnp.dot(in_weight[0:512, :], normed, preferred_element_type=F32)
        left_act = jax.nn.sigmoid(mixed[128:256]) * mixed[0:128]
        right_act = jax.nn.sigmoid(mixed[384:512]) * mixed[256:384]
        for t in range(GROUP):
            i = g * GROUP + t
            lanes = slice(t * LANES, (t + 1) * LANES)
            left_rows[pl.ds(i, LANES, stride=PITCH), :] = left_act[:, lanes]
            right_rows[pl.ds(i, LANES, stride=PITCH), :] = right_act[:, lanes]

    outer_product(0, range(16))
    fetch_weight.wait()
    fetch_pair.wait()
    groups = STEP_ROWS // GROUP
    share = 16 // (2 * groups)
    for step in range(steps):
        here = slice(step * STEP_ROWS, (step + 1) * STEP_ROWS)
        spread_rows(pair_rows, pair[:, here, :].astype(F32))
        for g in range(groups):
            normed = update(step, g)
            outer_product(step + 1, range(2 * g * share, (2 * g + 1) * share))
            activate(g, normed)
            outer_product(step + 1, range((2 * g + 1) * share, (2 * g + 2) * share))
        acts[:, 0, here, :] = gather_rows(left_rows)
        acts[:, 1, here, :] = gather_rows(right_rows)


def triangle_kernel(acts, out):
    def rows(block, side):
        return jnp.concatenate([acts[block * 8 + h, side] for h in range(8)], axis=1)

    for n in range(4):
        right = jnp.concatenate([rows(n * 4 + d, 1) for d in range(4)], axis=0)
        for m in range(4):
            left = jnp.concatenate([rows(m * 4 + d, 0) for d in range(4)], axis=0)
            product = contract_last(left, right).astype(BF16)
            for d in range(4):
                for h in range(2):
                    out[(m * 4 + d) * 8 + n * 2 + h] = product[d * 64:(d + 1) * 64, h * LANES:(h + 1) * LANES]


def finish_kernel(tri, mid, pair_normed, keep, gain, weight, gate_weight, out, tri_rows, out_rows):
    scale = keep[...].astype(F32) / 0.75
    first = pl.multiple_of(pl.program_id(0) * STEP_ROWS, STEP_ROWS)
    spread_rows(tri_rows, tri[:, pl.ds(first, STEP_ROWS), :].astype(F32))
    for g in range(STEP_ROWS // GROUP):
        x = jnp.concatenate(
            [tri_rows[pl.ds(g * GROUP + t, LANES, stride=PITCH), :] for t in range(GROUP)], axis=1
        )
        center = x - jnp.mean(x, axis=0, keepdims=True)
        spread = jnp.mean(center * center, axis=0, keepdims=True)
        normed = (center * lax.rsqrt(spread + EPS) * gain[...]).astype(BF16)
        update = jnp.dot(weight[...], normed, preferred_element_type=F32)
        gate = jnp.dot(
            gate_weight[512:640, :],
            jnp.concatenate([pair_normed[first + g * GROUP + t] for t in range(GROUP)], axis=1),
            preferred_element_type=F32,
        )
        update = jax.nn.sigmoid(gate).astype(BF16).astype(F32) * update
        for t in range(GROUP):
            i = g * GROUP + t
            out_rows[pl.ds(i, LANES, stride=PITCH), :] = (
                mid[first + i].astype(F32) + scale * update[:, t * LANES:(t + 1) * LANES]
            )
    out[...] = gather_rows(out_rows)


def whole(shape):
    return pl.BlockSpec(shape, lambda i: (0,) * len(shape))


def on_device(
    homolog_matrix_entering,
    attention_increment_undropped,
    retained_entries_indicator,
    pair,
    pair_keep_mask,
    homolog_standardizing_multiplier,
    left_right_factor_matrices,
    outer_product_output_weight,
    triangle_input_gain,
    triangle_input_weight,
    triangle_output_gain,
    triangle_output_weight,
):
    left_block, right_block = pl.pallas_call(
        operands_kernel,
        grid=(2,),
        out_shape=(jax.ShapeDtypeStruct((256, LANES), BF16), jax.ShapeDtypeStruct((256, LANES), BF16)),
        in_specs=[
            pl.BlockSpec((2, 4, ROWS, 256), lambda i: (0, i, 0, 0)),
            pl.BlockSpec((2, 4, ROWS, 256), lambda i: (0, i, 0, 0)),
            whole((ROWS, 256)),
            whole((1, 256)),
            whole((64, 256)),
        ],
        out_specs=(whole((256, LANES)), whole((256, LANES))),
        scratch_shapes=[pltpu.VMEM((512, LANES), F32)],
        compiler_params=params(16),
        name="operands",
    )(
        in_hbm(homolog_matrix_entering.reshape(2, 8, ROWS, 256)),
        in_hbm(attention_increment_undropped.reshape(2, 8, ROWS, 256)),
        in_hbm(retained_entries_indicator),
        in_hbm(homolog_standardizing_multiplier.reshape(1, 256)),
        in_hbm(left_right_factor_matrices.T),
    )
    both = ("dap", "ch")
    turn = [(d * 8 + h, (h * 2 + d % 2) * 8 + d // 2) for d in range(16) for h in range(8)]
    right_block = lax.ppermute(right_block[None], both, turn)
    raw = lax.optimization_barrier(
        (
            outer_product_output_weight,
            triangle_input_weight,
            triangle_input_gain.reshape(1, LANES),
            triangle_output_gain.reshape(1, LANES),
            triangle_output_weight,
            left_block,
        )
    )
    turned = pl.pallas_call(
        weights_kernel,
        out_shape=(
            jax.ShapeDtypeStruct((LANES, 1024), BF16),
            pltpu.VMEM((640, LANES), BF16),
            pltpu.VMEM((LANES, 1), F32),
            pltpu.VMEM((LANES, 1), F32),
            pltpu.VMEM((LANES, LANES), BF16),
        ),
        in_specs=[IN_VMEM] * 5,
        out_specs=(IN_VMEM,) * 5,
        compiler_params=pltpu.CompilerParams(vmem_limit_bytes=8 * MIB),
        name="weights",
    )(*[in_hbm(x) for x in raw[:5]])
    l_flip = lax.ppermute(left_block[None], "ch", [(i, i ^ 4) for i in range(8)])
    right_block, l_flip, turned = lax.optimization_barrier((right_block, l_flip, turned))
    r_flip = lax.ppermute(right_block, "dap", [(i, i ^ 2) for i in range(16)])
    l_pair = jnp.concatenate([left_block[None], l_flip], axis=0)
    l_quads = [l_pair] + [
        lax.ppermute(l_pair, "ch", [(i, (i & 4) | ((i + k) & 3)) for i in range(8)]) for k in range(1, 4)
    ]
    r_flip, l_quads = lax.optimization_barrier((r_flip, l_quads))
    r_pair = jnp.concatenate([right_block, r_flip], axis=0)
    quads = [r_pair] + [lax.ppermute(r_pair, "dap", [(i, (i + 4 * k) % 16) for i in range(16)]) for k in range(1, 4)]
    r_half = jnp.concatenate(quads, axis=0)
    r_other = lax.ppermute(r_half, "dap", [(i, i ^ 1) for i in range(16)])
    place = jnp.stack([lax.axis_index("dap"), lax.axis_index("ch")]).astype(jnp.int32)
    out_weight, in_weight, in_gain, tri_gain, tri_weight = turned
    acts, pair_mid, normed = pl.pallas_call(
        pair_kernel,
        out_shape=(
            pltpu.VMEM((LANES, 2, ROWS, LANES), BF16),
            pltpu.VMEM((ROWS, LANES, LANES), BF16),
            pltpu.VMEM((ROWS, LANES, LANES), BF16),
        ),
        in_specs=[pl.BlockSpec(memory_space=pltpu.SMEM)]
        + [IN_VMEM] * 6
        + [pl.BlockSpec(memory_space=pl.ANY)] * 2
        + [IN_VMEM] * 2,
        out_specs=(IN_VMEM,) * 3,
        scratch_shapes=[
            pltpu.VMEM((8, HIDDEN, 8, LANES), F32),
            pltpu.VMEM((ROWS * (HIDDEN + 8), LANES), F32),
            pltpu.VMEM((ROWS * HIDDEN, LANES), BF16),
            pltpu.VMEM((16, HIDDEN, 8, LANES), F32),
            pltpu.VMEM((LANES, HIDDEN * LANES), BF16),
            pltpu.VMEM((1024, STEP_ROWS * LANES), BF16),
            pltpu.VMEM((1024, STEP_ROWS * LANES), BF16),
            pltpu.VMEM((LANES * PITCH, LANES), F32),
            pltpu.VMEM((LANES * PITCH, LANES), F32),
            pltpu.VMEM((LANES * PITCH, LANES), F32),
            pltpu.VMEM((LANES, 1024), BF16),
            pltpu.VMEM((LANES, ROWS, LANES), BF16),
            pltpu.SemaphoreType.DMA,
            pltpu.SemaphoreType.DMA,
        ],
        compiler_params=pltpu.CompilerParams(vmem_limit_bytes=32 * MIB),
        name="pair_update",
    )(
        place, *[resident(x) for x in l_quads], resident(r_half), resident(r_other), in_hbm(pair),
        in_hbm(out_weight), resident(in_gain), resident(in_weight),
    )
    acts = lax.all_to_all(acts.reshape(LANES, LANES, LANES), both, 0, 0, tiled=True)

    tri = pl.pallas_call(
        triangle_kernel,
        out_shape=pltpu.VMEM((LANES, ROWS, LANES), BF16),
        in_specs=[IN_VMEM],
        out_specs=IN_VMEM,
        compiler_params=pltpu.CompilerParams(vmem_limit_bytes=16 * MIB),
        name="triangle",
    )(resident(acts.reshape(LANES, 2, ROWS, LANES)))
    tri = lax.all_to_all(tri, both, 0, 0, tiled=True)

    return pl.pallas_call(
        finish_kernel,
        grid=(ROWS // STEP_ROWS,),
        out_shape=jax.ShapeDtypeStruct((LANES, ROWS, LANES), BF16),
        in_specs=[IN_VMEM] * 7,
        out_specs=pl.BlockSpec((LANES, STEP_ROWS, LANES), lambda i: (0, i, 0)),
        scratch_shapes=[pltpu.VMEM((LANES * PITCH, LANES), F32)] * 2,
        compiler_params=params(20),
        name="finish",
    )(
        resident(tri), resident(pair_mid), resident(normed), pair_keep_mask,
        resident(tri_gain), resident(tri_weight), resident(in_weight),
    )


def solution(mesh):
    placed = (
        P("ch", "dap", None),
        P("ch", "dap", None),
        P("dap", None),
        P(None, "dap", "ch"),
        P(None, "ch"),
        P(),
        P(),
        P(),
        P(),
        P(),
        P(),
        P(),
    )
    return jax.shard_map(
        on_device, mesh=mesh, in_specs=placed, out_specs=P(None, "dap", "ch"), check_vma=False
    )
```

```python
import jax
import jax.numpy as jnp
from jax import lax
from jax.experimental import pallas as pl
from jax.experimental.pallas import tpu as pltpu
from jax.sharding import PartitionSpec as P

F32 = jnp.float32
BF16 = jnp.bfloat16
EPS = 1e-05
MIB = 1024 * 1024
HIDDEN = 32
LANES = 128
ROWS = 64
STEP_ROWS = 16
PITCH = 24
GROUP = 8


def contract_last(a, b):
    return lax.dot_general(a, b, (((1,), (1,)), ((), ())), preferred_element_type=F32)


def params(mib):
    return pltpu.CompilerParams(vmem_limit_bytes=mib * MIB, dimension_semantics=("arbitrary",))


def resident(x):
    return pltpu.with_memory_space_constraint(x, pltpu.VMEM)


def in_hbm(x):
    return pltpu.with_memory_space_constraint(x, pltpu.HBM)


IN_VMEM = pl.BlockSpec(memory_space=pltpu.VMEM)


def operands_kernel(homolog, increment, keep, gain, weight, left_out, right_out, rows_out):
    step = pl.program_id(0)
    scale = keep[...].astype(F32) / 0.85
    for t in range(4):
        parts = []
        for half in range(2):
            x = homolog[half, t].astype(F32) + scale * increment[half, t].astype(F32)
            center = x - jnp.mean(x, axis=-1, keepdims=True)
            spread = jnp.mean(center * center, axis=-1, keepdims=True)
            parts.append((center * lax.rsqrt(spread + EPS) * gain[...]).astype(BF16))
        projected = contract_last(weight[...], jnp.concatenate(parts, axis=0))
        rows_out[pl.ds(step * 4 + t, 64, stride=8), :] = projected

    @pl.when(step == pl.num_programs(0) - 1)
    def _():
        left_out[...] = rows_out[0:256, :].astype(BF16)
        right_out[...] = rows_out[256:512, :].astype(BF16)


def spread_rows(rows, values):
    for c in range(LANES):
        rows[c * PITCH:c * PITCH + STEP_ROWS, :] = values[c]


def gather_rows(rows):
    return rows[...].reshape(LANES, PITCH, LANES)[:, :STEP_ROWS].astype(BF16)


def weights_kernel(
    out_weight, in_weight, in_gain, tri_gain, tri_weight,
    out_turned, in_turned, in_column, tri_column, tri_turned,
):
    w = out_weight[...].astype(F32).reshape(HIDDEN, HIDDEN, LANES)
    for d in range(HIDDEN // 4):
        rows = jnp.concatenate([w[:, 4 * d + q, :] for q in range(4)], axis=0)
        out_turned[:, d * LANES:(d + 1) * LANES] = rows.T.astype(BF16)
    for k in range(5):
        in_turned[k * LANES:(k + 1) * LANES, :] = in_weight[:, k * LANES:(k + 1) * LANES].astype(F32).T.astype(BF16)
    tri_turned[...] = tri_weight[...].astype(F32).T.astype(BF16)
    in_column[...] = jnp.broadcast_to(in_gain[...], (8, LANES)).T[:, 0:1]
    tri_column[...] = jnp.broadcast_to(tri_gain[...], (8, LANES)).T[:, 0:1]


def turn_left(place, quads, left, parts, rows):
    for k, blocks in enumerate(quads):
        for q in range(4):
            spot = ((place[1] & 4) | ((place[1] - q) & 3)) ^ (4 * k)
            parts[spot] = blocks[q].astype(F32).reshape(HIDDEN, 8, LANES)
    for c in range(HIDDEN):
        turned = parts[:, c].reshape(64, LANES).T
        rows[pl.ds(c, ROWS, stride=HIDDEN + 8), :] = jnp.concatenate([turned[:64], turned[64:]], axis=1)
    left[...] = rows[...].reshape(ROWS, HIDDEN + 8, LANES)[:, :HIDDEN].reshape(ROWS * HIDDEN, LANES).astype(BF16)


def pair_kernel(
    place, l0, l1, r_half, r_other, pair_far, out_weight, gain, in_weight,
    acts, mid_out, normed_out,
    l_parts, l_rows, left, r_parts, right, outer_a, outer_b, pair_rows, left_rows, right_rows,
    weight_here, pair, weight_sem, pair_sem,
):
    fetch_weight = pltpu.make_async_copy(out_weight, weight_here, weight_sem)
    fetch_pair = pltpu.make_async_copy(pair_far, pair, pair_sem)
    fetch_weight.start()
    fetch_pair.start()
    turn_left(place, (l0, l1), left, l_parts, l_rows)
    for q in range(8):
        for other, blocks in enumerate((r_half, r_other)):
            spot = (((place[0] ^ other) - 4 * (q // 2)) & 15) ^ (2 * (q % 2))
            r_parts[(spot & 1) * 8 + (spot >> 1)] = blocks[q].astype(F32).reshape(HIDDEN, 8, LANES)
    low = lax.broadcasted_iota(jnp.int32, (64, LANES), 1) < 64
    for d in range(HIDDEN):
        a0 = r_parts[0:8, d].reshape(64, LANES)
        a1 = r_parts[8:16, d].reshape(64, LANES)
        first = jnp.where(low, a0, pltpu.roll(a1, 64, 1))
        second = jnp.where(low, pltpu.roll(a0, 64, 1), a1)
        right[:, d * LANES:(d + 1) * LANES] = jnp.concatenate([first, second], axis=0).astype(BF16)

    outers = (outer_a, outer_b)
    steps = ROWS // STEP_ROWS

    def outer_product(step, chunks):
        if step >= steps:
            return
        outer = outers[step % 2]
        rows = left[step * STEP_ROWS * HIDDEN:(step + 1) * STEP_ROWS * HIDDEN, :]
        for n in chunks:
            product = jnp.dot(rows, right[:, n * 256:(n + 1) * 256], preferred_element_type=F32).astype(BF16)
            for i in range(STEP_ROWS):
                for q in range(2):
                    d = 2 * n + q
                    outer[d * HIDDEN:(d + 1) * HIDDEN, i * LANES:(i + 1) * LANES] = product[
                        i * HIDDEN:(i + 1) * HIDDEN, q * LANES:(q + 1) * LANES
                    ]

    def update(step, g):
        mean_part = jnp.dot(
            weight_here[...], outers[step % 2][:, g * GROUP * LANES:(g + 1) * GROUP * LANES],
            preferred_element_type=F32,
        ) * (1.0 / 128.0)
        base = jnp.concatenate(
            [pair_rows[pl.ds(g * GROUP + t, LANES, stride=PITCH), :] for t in range(GROUP)], axis=1
        )
        mid = (base + mean_part).astype(BF16)
        x = mid.astype(F32)
        center = x - jnp.mean(x, axis=0, keepdims=True)
        spread = jnp.mean(center * center, axis=0, keepdims=True)
        normed = (center * lax.rsqrt(spread + EPS) * gain[...]).astype(BF16)
        for t in range(GROUP):
            i = step * STEP_ROWS + g * GROUP + t
            mid_out[i] = mid[:, t * LANES:(t + 1) * LANES]
            normed_out[i] = normed[:, t * LANES:(t + 1) * LANES]
        return normed

    def activate(g, normed):
        mixed = jnp.dot(in_weight[0:512, :], normed, preferred_element_type=F32)
        left_act = jax.nn.sigmoid(mixed[128:256]) * mixed[0:128]
        right_act = jax.nn.sigmoid(mixed[384:512]) * mixed[256:384]
        for t in range(GROUP):
            i = g * GROUP + t
            lanes = slice(t * LANES, (t + 1) * LANES)
            left_rows[pl.ds(i, LANES, stride=PITCH), :] = left_act[:, lanes]
            right_rows[pl.ds(i, LANES, stride=PITCH), :] = right_act[:, lanes]

    outer_product(0, range(16))
    fetch_weight.wait()
    fetch_pair.wait()
    groups = STEP_ROWS // GROUP
    share = 16 // (2 * groups)
    for step in range(steps):
        here = slice(step * STEP_ROWS, (step + 1) * STEP_ROWS)
        spread_rows(pair_rows, pair[:, here, :].astype(F32))
        for g in range(groups):
            normed = update(step, g)
            outer_product(step + 1, range(2 * g * share, (2 * g + 1) * share))
            activate(g, normed)
            outer_product(step + 1, range((2 * g + 1) * share, (2 * g + 2) * share))
        acts[:, 0, here, :] = gather_rows(left_rows)
        acts[:, 1, here, :] = gather_rows(right_rows)


def triangle_kernel(acts, out):
    def rows(block, side):
        return jnp.concatenate([acts[block * 8 + h, side] for h in range(8)], axis=1)

    for n in range(4):
        right = jnp.concatenate([rows(n * 4 + d, 1) for d in range(4)], axis=0)
        for m in range(4):
            left = jnp.concatenate([rows(m * 4 + d, 0) for d in range(4)], axis=0)
            product = contract_last(left, right).astype(BF16)
            for d in range(4):
                for h in range(2):
                    out[(m * 4 + d) * 8 + n * 2 + h] = product[d * 64:(d + 1) * 64, h * LANES:(h + 1) * LANES]


def finish_kernel(tri, mid, pair_normed, keep, gain, weight, gate_weight, out, tri_rows, out_rows):
    scale = keep[...].astype(F32) / 0.75
    first = pl.multiple_of(pl.program_id(0) * STEP_ROWS, STEP_ROWS)
    spread_rows(tri_rows, tri[:, pl.ds(first, STEP_ROWS), :].astype(F32))
    for g in range(STEP_ROWS // GROUP):
        x = jnp.concatenate(
            [tri_rows[pl.ds(g * GROUP + t, LANES, stride=PITCH), :] for t in range(GROUP)], axis=1
        )
        center = x - jnp.mean(x, axis=0, keepdims=True)
        spread = jnp.mean(center * center, axis=0, keepdims=True)
        normed = (center * lax.rsqrt(spread + EPS) * gain[...]).astype(BF16)
        update = jnp.dot(weight[...], normed, preferred_element_type=F32)
        gate = jnp.dot(
            gate_weight[512:640, :],
            jnp.concatenate([pair_normed[first + g * GROUP + t] for t in range(GROUP)], axis=1),
            preferred_element_type=F32,
        )
        update = jax.nn.sigmoid(gate).astype(BF16).astype(F32) * update
        for t in range(GROUP):
            i = g * GROUP + t
            out_rows[pl.ds(i, LANES, stride=PITCH), :] = (
                mid[first + i].astype(F32) + scale * update[:, t * LANES:(t + 1) * LANES]
            )
    out[...] = gather_rows(out_rows)


def whole(shape):
    return pl.BlockSpec(shape, lambda i: (0,) * len(shape))


def on_device(
    homolog_matrix_entering,
    attention_increment_undropped,
    retained_entries_indicator,
    pair,
    pair_keep_mask,
    homolog_standardizing_multiplier,
    left_right_factor_matrices,
    outer_product_output_weight,
    triangle_input_gain,
    triangle_input_weight,
    triangle_output_gain,
    triangle_output_weight,
):
    left_block, right_block = pl.pallas_call(
        operands_kernel,
        grid=(2,),
        out_shape=(jax.ShapeDtypeStruct((256, LANES), BF16), jax.ShapeDtypeStruct((256, LANES), BF16)),
        in_specs=[
            pl.BlockSpec((2, 4, ROWS, 256), lambda i: (0, i, 0, 0)),
            pl.BlockSpec((2, 4, ROWS, 256), lambda i: (0, i, 0, 0)),
            whole((ROWS, 256)),
            whole((1, 256)),
            whole((64, 256)),
        ],
        out_specs=(whole((256, LANES)), whole((256, LANES))),
        scratch_shapes=[pltpu.VMEM((512, LANES), F32)],
        compiler_params=params(16),
        name="operands",
    )(
        in_hbm(homolog_matrix_entering.reshape(2, 8, ROWS, 256)),
        in_hbm(attention_increment_undropped.reshape(2, 8, ROWS, 256)),
        in_hbm(retained_entries_indicator),
        in_hbm(homolog_standardizing_multiplier.reshape(1, 256)),
        in_hbm(left_right_factor_matrices.T),
    )
    both = ("dap", "ch")
    turn = [(d * 8 + h, (h * 2 + d % 2) * 8 + d // 2) for d in range(16) for h in range(8)]
    right_block = lax.ppermute(right_block[None], both, turn)
    raw = lax.optimization_barrier(
        (
            outer_product_output_weight,
            triangle_input_weight,
            triangle_input_gain.reshape(1, LANES),
            triangle_output_gain.reshape(1, LANES),
            triangle_output_weight,
            left_block,
        )
    )
    turned = pl.pallas_call(
        weights_kernel,
        out_shape=(
            jax.ShapeDtypeStruct((LANES, 1024), BF16),
            pltpu.VMEM((640, LANES), BF16),
            pltpu.VMEM((LANES, 1), F32),
            pltpu.VMEM((LANES, 1), F32),
            pltpu.VMEM((LANES, LANES), BF16),
        ),
        in_specs=[IN_VMEM] * 5,
        out_specs=(IN_VMEM,) * 5,
        compiler_params=pltpu.CompilerParams(vmem_limit_bytes=8 * MIB),
        name="weights",
    )(*[in_hbm(x) for x in raw[:5]])
    l_row = [left_block[None]] + [
        lax.ppermute(left_block[None], "ch", [(i, (i & 4) | ((i + k) & 3)) for i in range(8)]) for k in range(1, 4)
    ]
    right_block, l_row, turned = lax.optimization_barrier((right_block, l_row, turned))
    r_flip = lax.ppermute(right_block, "dap", [(i, i ^ 2) for i in range(16)])
    l_own = jnp.concatenate(l_row, axis=0)
    r_flip, l_own = lax.optimization_barrier((r_flip, l_own))
    l_far = lax.ppermute(l_own, "ch", [(i, i ^ 4) for i in range(8)])
    r_pair = jnp.concatenate([right_block, r_flip], axis=0)
    quads = [r_pair] + [lax.ppermute(r_pair, "dap", [(i, (i + 4 * k) % 16) for i in range(16)]) for k in range(1, 4)]
    quads, l_far = lax.optimization_barrier((quads, l_far))
    l_quads = [l_own, l_far]
    r_half = jnp.concatenate(quads, axis=0)
    r_other = lax.ppermute(r_half, "dap", [(i, i ^ 1) for i in range(16)])
    place = jnp.stack([lax.axis_index("dap"), lax.axis_index("ch")]).astype(jnp.int32)
    out_weight, in_weight, in_gain, tri_gain, tri_weight = turned
    acts, pair_mid, normed = pl.pallas_call(
        pair_kernel,
        out_shape=(
            pltpu.VMEM((LANES, 2, ROWS, LANES), BF16),
            pltpu.VMEM((ROWS, LANES, LANES), BF16),
            pltpu.VMEM((ROWS, LANES, LANES), BF16),
        ),
        in_specs=[pl.BlockSpec(memory_space=pltpu.SMEM)]
        + [IN_VMEM] * 4
        + [pl.BlockSpec(memory_space=pl.ANY)] * 2
        + [IN_VMEM] * 2,
        out_specs=(IN_VMEM,) * 3,
        scratch_shapes=[
            pltpu.VMEM((8, HIDDEN, 8, LANES), F32),
            pltpu.VMEM((ROWS * (HIDDEN + 8), LANES), F32),
            pltpu.VMEM((ROWS * HIDDEN, LANES), BF16),
            pltpu.VMEM((16, HIDDEN, 8, LANES), F32),
            pltpu.VMEM((LANES, HIDDEN * LANES), BF16),
            pltpu.VMEM((1024, STEP_ROWS * LANES), BF16),
            pltpu.VMEM((1024, STEP_ROWS * LANES), BF16),
            pltpu.VMEM((LANES * PITCH, LANES), F32),
            pltpu.VMEM((LANES * PITCH, LANES), F32),
            pltpu.VMEM((LANES * PITCH, LANES), F32),
            pltpu.VMEM((LANES, 1024), BF16),
            pltpu.VMEM((LANES, ROWS, LANES), BF16),
            pltpu.SemaphoreType.DMA,
            pltpu.SemaphoreType.DMA,
        ],
        compiler_params=pltpu.CompilerParams(vmem_limit_bytes=32 * MIB),
        name="pair_update",
    )(
        place, *[resident(x) for x in l_quads], resident(r_half), resident(r_other), in_hbm(pair),
        in_hbm(out_weight), resident(in_gain), resident(in_weight),
    )
    acts = lax.all_to_all(acts.reshape(LANES, LANES, LANES), both, 0, 0, tiled=True)

    tri = pl.pallas_call(
        triangle_kernel,
        out_shape=pltpu.VMEM((LANES, ROWS, LANES), BF16),
        in_specs=[IN_VMEM],
        out_specs=IN_VMEM,
        compiler_params=pltpu.CompilerParams(vmem_limit_bytes=16 * MIB),
        name="triangle",
    )(resident(acts.reshape(LANES, 2, ROWS, LANES)))
    tri = lax.all_to_all(tri, both, 0, 0, tiled=True)

    return pl.pallas_call(
        finish_kernel,
        grid=(ROWS // STEP_ROWS,),
        out_shape=jax.ShapeDtypeStruct((LANES, ROWS, LANES), BF16),
        in_specs=[IN_VMEM] * 7,
        out_specs=pl.BlockSpec((LANES, STEP_ROWS, LANES), lambda i: (0, i, 0)),
        scratch_shapes=[pltpu.VMEM((LANES * PITCH, LANES), F32)] * 2,
        compiler_params=params(20),
        name="finish",
    )(
        resident(tri), resident(pair_mid), resident(normed), pair_keep_mask,
        resident(tri_gain), resident(tri_weight), resident(in_weight),
    )


def solution(mesh):
    placed = (
        P("ch", "dap", None),
        P("ch", "dap", None),
        P("dap", None),
        P(None, "dap", "ch"),
        P(None, "ch"),
        P(),
        P(),
        P(),
        P(),
        P(),
        P(),
        P(),
    )
    return jax.shard_map(
        on_device, mesh=mesh, in_specs=placed, out_specs=P(None, "dap", "ch"), check_vma=False
    )
```
